32 devices in a mesh: sta: 2 (over x), tm: 16 (over z, y, core).
Axes of the slice: x: 2, y: 2, z: 4, core: 2. Of those that a mesh axis runs over, the one named last changes fastest.
Arguments:
- record: bfloat16 [96, 12288], P('sta', 'tm')
- templates: bfloat16 [64, 96, 512], P('tm', 'sta'), may hold values from -6 to 6
- shifts: int32 [96], P('sta'), may hold values from 0 to 255, as said below
- live_mask: int32 [96], P('sta'), may hold values 0 or 1
- plan: int32 [64], replicated, may hold values from 0 to 63, each once
Outputs:
- stacks: float32 [64, 12288], P('sta', 'tm')
The draws below stay inside these ranges and needn't reach their ends.
Inputs may be any that keep to these rules, and one draw needn't show every extreme that they name: `shifts`: some channel has the shift 256 - 1. `plan`: each bank slot appears once.
All inputs are finite; a program needn't handle non-finite values. No bound on the sum of `live_mask` on one device may be relied on, other than what follows from the above.
Results may differ from the reference program's by a relative error of at most 0.0003.
Values may be sent and summed in bfloat16 or wider, within the bound.
No kernel may reach another device: no remote copies, remote signals or barrier semaphores. Data moves between devices by JAX's collectives and lax.ppermute only.
A program may use at most 64 MiB of HBM per device.

```python
import math
import jax
import jax.numpy as jnp
from jax import lax

TEMPLATES = 64
CHANNELS = 96
TAPS = 512
MAX_SHIFT = 256
SAMPLES = 12288


def draw_record(key, part):
    key_base, key_chan, key_env = jax.random.split(key, 3)
    noise_base = jax.random.normal(key_base, (CHANNELS, SAMPLES), jnp.float32)
    chan_scale = jnp.exp(jax.random.uniform(key_chan, (CHANNELS, 1), jnp.float32) * math.log(10.0))
    envelope = jnp.exp(jax.random.uniform(key_env, (CHANNELS, SAMPLES // 64), jnp.float32, -1.0, 1.0) * math.log(3.0))
    envelope = jnp.repeat(envelope, 64, axis=1)
    return (noise_base * chan_scale * envelope).astype(jnp.bfloat16)


def draw_shifts(key, part):
    key_lags, key_pin = jax.random.split(key, 2)
    lag_draw = jax.random.randint(key_lags, (CHANNELS,), 0, MAX_SHIFT)
    pinned = jax.random.randint(key_pin, (), 0, CHANNELS)
    return lag_draw.at[pinned].set(MAX_SHIFT - 1).astype(jnp.int32)


def touch_ends(result, own_key, least, high):
    extent = result.shape
    place = [jax.random.randint(jax.random.fold_in(own_key, axis), (), 0, extent[axis]) for axis in range(len(extent))]
    result = result.at[tuple(place)].set(least)
    longest = extent.index(max(extent))
    place[longest] = (place[longest] + 1) % extent[longest]
    return result.at[tuple(place)].set(high)


def level_of(stream_key, extent, pieces, smallest, top_value):
    gain, own = 1.0, jax.random.fold_in(stream_key, 6)
    for axis_at, blocks in pieces:
        steps = jnp.exp(jax.random.uniform(jax.random.fold_in(own, axis_at), (blocks,), jnp.float32, smallest / len(pieces), top_value / len(pieces)))
        gain = gain * jnp.repeat(steps, extent[axis_at] // blocks).reshape([-1 if axis == axis_at else 1 for axis in range(len(extent))])
    return gain


def centred(own_key, extent, width, reach, pieces=(), held_as=jnp.bfloat16):
    values = jax.random.normal(own_key, extent, jnp.float32) * width
    if len(pieces) > 0:
        values = level_of(own_key, extent, pieces, -0.22, 0.18) * values
    return jnp.clip(values, min=-reach, max=reach).astype(held_as)


def setup_inputs(seed: int = 0) -> dict:
    keys = jax.random.split(jax.random.key(seed), 6)
    record = draw_record(jax.random.fold_in(keys[5], 71), 0)
    templates = centred(keys[1], (TEMPLATES, CHANNELS, TAPS), 1.0, 6.0, ((0, 16), (1, 2)))
    shifts = draw_shifts(jax.random.fold_in(keys[5], 71), 0)
    live_mask = touch_ends((jax.random.randint(keys[3], (CHANNELS,), 0, 4) < 3).astype(jnp.int32), jax.random.fold_in(keys[3], 1), 0, 1)
    plan = jax.random.permutation(keys[4], TEMPLATES).astype(jnp.int32)
    return dict(record=record, templates=templates, shifts=shifts, live_mask=live_mask, plan=plan)


def reference(record, templates, shifts, live_mask, plan):
    signal = record.astype(jnp.float32)
    padded = jnp.pad(signal, ((0, 0), (0, MAX_SHIFT + TAPS)))
    total_len = SAMPLES + TAPS
    overall = math.sqrt(TAPS / CHANNELS)

    def add_channel(chan_idx, running):
        signal_row = lax.dynamic_index_in_dim(padded, chan_idx, 0, keepdims=False)
        window = lax.dynamic_slice_in_dim(signal_row, shifts[chan_idx].astype(jnp.int32), total_len)
        copies = jnp.tile(window, TAPS + 1)
        hankel = copies[:TAPS * (total_len + 1)].reshape(TAPS, total_len + 1)[:, :SAMPLES]
        panel_rows = lax.dynamic_index_in_dim(templates, chan_idx, 1, keepdims=False).astype(jnp.float32)
        products = jnp.dot(panel_rows, hankel, precision=lax.Precision.HIGHEST)
        energy = lax.optimization_barrier(jnp.sum(hankel * hankel, axis=0))
        norm_vals = jnp.sqrt(lax.optimization_barrier(jnp.sum(panel_rows * panel_rows, axis=1)) + 1e-06)
        weighting = live_mask[chan_idx].astype(jnp.float32) * overall / norm_vals
        return running + products * weighting[:, None] * lax.rsqrt(energy + 1e-06)[None, :]
    running = lax.fori_loop(0, CHANNELS, add_channel, jnp.zeros((TEMPLATES, SAMPLES), jnp.float32))
    return jnp.take(running, plan, axis=0)
```

```python
import functools
import math

import jax
import jax.numpy as jnp
from jax import lax
from jax.experimental import pallas as pl
from jax.experimental.pallas import tpu as pltpu
from jax.sharding import PartitionSpec as P

CHANNELS = 96
LANES = 128
MAX_SHIFT = 256


def passed_along(shard, axis, by):
    count = lax.axis_size(axis)
    pairs = [(i, i + by) for i in range(count) if 0 <= i + by < count]
    return lax.ppermute(shard, axis, pairs)


def rolled_left(values, by, axis=1):
    width = values.shape[axis]
    return pltpu.roll(values, (width - by) % width, axis)


def corr_kernel(pieces, outs, shifts, live, rows, record, rim, *rest):
    banks, out_refs = rest[:pieces], rest[pieces : pieces + outs]
    ext, scale, taps_f32, hankel, acc = rest[pieces + outs :]
    chans, span = record.shape
    taps = banks[0].shape[2]
    per_bank = banks[0].shape[0]
    tmpl = per_bank * pieces
    width, long = 2 * span, span + taps
    blocks = taps // LANES
    overall = math.sqrt(taps / CHANNELS)

    for first in range(0, chans, 16):
        part = pl.ds(first, 16)
        both = jnp.concatenate([record[part, :], rim[part, :]], axis=1).astype(jnp.float32)
        ext[part, :] = both
        window, reach = both * both, 1
        while reach < taps:
            window = window + rolled_left(window, reach)
            reach *= 2
        scale[part, :] = lax.rsqrt(window[:, : scale.shape[1]] + 1e-06)

    for idx, bank in enumerate(banks):
        flat = bank[...].reshape(per_bank * chans, taps)
        for m in range(blocks):
            taps_f32[m, pl.ds(idx * per_bank * chans, per_bank * chans), :] = flat[
                :, m * LANES : (m + 1) * LANES
            ].astype(jnp.float32)

    acc[...] = jnp.zeros_like(acc)
    flip = 7 - lax.broadcasted_iota(jnp.int32, (8, long), 0)

    def add_channel(chan, carry):
        lag = shifts[chan]
        row = pltpu.roll(ext[pl.ds(chan, 1), :], lax.rem(width - lag, width), 1)[:, :long]
        span_scale = scale.shape[1]
        level = pltpu.roll(
            scale[pl.ds(chan, 1), :], lax.rem(span_scale - lag, span_scale), 1
        )[:, :span]
        eight = pltpu.roll(
            jnp.broadcast_to(row, (8, long)), long - 7, 1, stride=1, stride_axis=0
        )
        eight = jnp.take_along_axis(eight, flip, axis=0, mode="promise_in_bounds")
        base = jnp.concatenate([eight, rolled_left(eight, 8)], axis=0).astype(jnp.bfloat16)
        keep = hankel.shape[1]
        for group in range(LANES // 16):
            hankel[pl.ds(16 * group, 16), :] = rolled_left(base, 16 * group)[:, :keep]
        panel = jnp.concatenate(
            [taps_f32[m, pl.ds(chan, tmpl, stride=chans), :] for m in range(blocks)], axis=1
        )
        power = jnp.sum(panel * panel, axis=1, keepdims=True)
        weight = live[chan].astype(jnp.float32) * overall * lax.rsqrt(power + 1e-06)
        stacked = jnp.concatenate(
            [hankel[:, m * LANES : m * LANES + span] for m in range(blocks)], axis=0
        )
        product = jnp.dot(
            panel.astype(jnp.bfloat16), stacked, preferred_element_type=jnp.float32
        )
        acc[...] += product * level * weight
        return carry

    lax.fori_loop(0, chans, add_channel, 0)
    share = tmpl // outs
    for j, out in enumerate(out_refs):
        for p in range(share):
            out[pl.ds(p, 1), :] = acc[pl.ds(rows[j * share + p], 1), :]


def correlate(banks, record, rim, shifts, live, rows, outs):
    chans, span = record.shape
    per_bank, _, taps = banks[0].shape
    tmpl = per_bank * len(banks)
    smem = pl.BlockSpec(memory_space=pltpu.SMEM)
    vmem = pl.BlockSpec(memory_space=pltpu.VMEM)
    return pl.pallas_call(
        functools.partial(corr_kernel, len(banks), outs),
        out_shape=[jax.ShapeDtypeStruct((tmpl // outs, span), jnp.float32)] * outs,
        in_specs=[smem] * 3 + [vmem] * (2 + len(banks)),
        out_specs=[vmem] * outs,
        scratch_shapes=[
            pltpu.VMEM((chans, 2 * span), jnp.float32),
            pltpu.VMEM((chans, span + MAX_SHIFT), jnp.float32),
            pltpu.VMEM((taps // LANES, tmpl * chans, LANES), jnp.float32),
            pltpu.VMEM((LANES, span + taps - LANES), jnp.bfloat16),
            pltpu.VMEM((tmpl, span), jnp.float32),
        ],
        compiler_params=pltpu.CompilerParams(vmem_limit_bytes=40 * 1024 * 1024),
        cost_estimate=pl.CostEstimate(
            flops=2 * tmpl * chans * taps * span,
            bytes_accessed=2 * tmpl * chans * taps,
            transcendentals=0,
        ),
    )(shifts, live, rows, record, rim, *banks)


def padded(values, axis, multiple):
    extra = -values.shape[axis] % multiple
    if extra == 0:
        return values
    widths = [(0, extra if i == axis else 0) for i in range(values.ndim)]
    return jnp.pad(values, widths)


def per_device(record, templates, shifts, live_mask, plan):
    record, shifts, live_mask = (padded(v, 0, 16) for v in (record, shifts, live_mask))
    templates = padded(templates, 1, 16)
    groups = lax.axis_size("sta")
    own = lax.axis_index("sta")
    rim = passed_along(record, "tm", -1)
    bank_all = lax.all_gather(templates, "tm", axis=0, tiled=True)
    share = plan.shape[0] // groups
    rows = jnp.roll(plan, -own * share)
    halves = correlate([bank_all], record, rim, shifts, live_mask, rows, groups)
    total = halves[0]
    for by in range(1, groups):
        pairs = [(i, (i + by) % groups) for i in range(groups)]
        total = total + lax.ppermute(halves[by], "sta", pairs)
    return total


def solution(mesh):
    placed = (P("sta", "tm"), P("tm", "sta", None), P("sta"), P("sta"), P())
    return jax.shard_map(
        per_device, mesh=mesh, in_specs=placed, out_specs=P("sta", "tm"), check_vma=False
    )
```

```python
import functools
import math

import jax
import jax.numpy as jnp
import numpy as np
from jax import lax
from jax.experimental import pallas as pl
from jax.experimental.pallas import tpu as pltpu
from jax.sharding import PartitionSpec as P

LANES = 128
GROUP = 16
MAX_SHIFT = 256
SMEM = pl.BlockSpec(memory_space=pltpu.SMEM)


def rolled_left(values, by):
    width = values.shape[1]
    return pltpu.roll(values, (width - by) % width, 1)


def padded(values, axis, multiple):
    extra = -values.shape[axis] % multiple
    if extra == 0:
        return values
    widths = [(0, extra if i == axis else 0) for i in range(values.ndim)]
    return jnp.pad(values, widths)


def prep_kernel(shifts, *refs):
    segs = len(refs[:-4]) // 2
    blocks, (base, level, lines, flat) = refs[:-4], refs[-4:]
    chans, span = blocks[0].shape
    taps = base.shape[3] - span
    width, long = 2 * span, span + taps
    for seg in range(segs):
        for first in range(0, chans, GROUP):
            part = pl.ds(first, GROUP)
            both = jnp.concatenate(
                [blocks[2 * seg][part, :], blocks[2 * seg + 1][part, :]], axis=1
            ).astype(jnp.float32)
            window, reach = both * both, 1
            while reach < taps:
                window = window + rolled_left(window, reach)
                reach *= 2
            rate = lax.rsqrt(window + 1e-06)
            for m in range(width // LANES):
                cols = slice(m * LANES, (m + 1) * LANES)
                flat[m, pl.ds(8 * first + seg, GROUP, stride=8), :] = both[:, cols]
                flat[m, pl.ds(8 * first + segs + seg, GROUP, stride=8), :] = rate[:, cols]

    flip = 7 - lax.broadcasted_iota(jnp.int32, (8, long), 0)

    def one(chan, slot):
        lag = shifts[chan]
        rows = pl.ds(pl.multiple_of(chan * 8, 8), 8)
        held = jnp.concatenate([flat[m, rows, :] for m in range(width // LANES)], axis=1)
        lines[slot] = pltpu.roll(held, lax.rem(width - lag, width), 1)[:, :long]
        for seg in range(segs):
            level[seg, pl.ds(chan, 1), :] = lines[slot, pl.ds(segs + seg, 1), :span]
            eight = pltpu.roll(
                jnp.broadcast_to(lines[slot, pl.ds(seg, 1), :], (8, long)),
                long - 7,
                1,
                stride=1,
                stride_axis=0,
            )
            eight = jnp.take_along_axis(eight, flip, axis=0, mode="promise_in_bounds")
            base[seg, chan] = jnp.concatenate([eight, rolled_left(eight, 8)], axis=0).astype(
                jnp.bfloat16
            )

    unroll = 4

    def body(step, carry):
        for u in range(unroll):
            one(step * unroll + u, u)
        return carry

    lax.fori_loop(0, chans // unroll, body, 0)


def prepare(shifts, blocks, taps):
    segs = len(blocks) // 2
    chans, span = blocks[0].shape
    whole = [pl.BlockSpec((chans, span), lambda i: (0, 0))] * len(blocks)
    return pl.pallas_call(
        prep_kernel,
        grid=(1,),
        out_shape=[
            jax.ShapeDtypeStruct((segs, chans, 16, span + taps), jnp.bfloat16),
            jax.ShapeDtypeStruct((segs, chans, span), jnp.float32),
        ],
        in_specs=[SMEM] + whole,
        out_specs=[
            pl.BlockSpec((segs, chans, 16, span + taps), lambda i: (0, 0, 0, 0)),
            pl.BlockSpec((segs, chans, span), lambda i: (0, 0, 0)),
        ],
        scratch_shapes=[
            pltpu.VMEM((4, 8, span + taps), jnp.float32),
            pltpu.VMEM((2 * span // LANES, chans * 8, LANES), jnp.float32),
        ],
        compiler_params=pltpu.CompilerParams(vmem_limit_bytes=40 * 1024 * 1024),
        cost_estimate=pl.CostEstimate(flops=1, bytes_accessed=10**7, transcendentals=0),
    )(shifts, *blocks)


def corr_kernel(pieces, first, overall, live, base, level, *refs):
    banks, (before, total, flat) = refs[:pieces], refs[pieces:]
    per, group, taps = banks[0].shape
    tmpl = per * pieces
    segs, span = level.shape[0], level.shape[2]
    parts, half = taps // LANES, 2 * LANES
    step = pl.program_id(0)

    @pl.when(step == 0)
    def _():
        if before is None:
            total[...] = jnp.zeros_like(total)
        else:
            total[...] = before[...]

    for idx, bank in enumerate(banks):
        rows = bank[...].reshape(per * group, taps).astype(jnp.float32)
        for m in range(parts):
            flat[m, pl.ds(idx * per * group, per * group), :] = rows[
                :, m * LANES : (m + 1) * LANES
            ]

    def one(chan):
        panel = jnp.concatenate(
            [flat[m, pl.ds(chan, tmpl, stride=group), :] for m in range(parts)], axis=1
        )
        power = jnp.sum(panel * panel, axis=1, keepdims=True)
        alive = live[first + step * group + chan].astype(jnp.float32)
        weight = alive * overall * lax.rsqrt(power + 1e-06)
        panel = panel.astype(jnp.bfloat16)
        stacked = jnp.concatenate(
            [panel[:, k * half : (k + 1) * half] for k in range(taps // half)], axis=0
        )
        for seg in range(segs):
            rows = base[seg, chan]
            sheet = jnp.concatenate(
                [rolled_left(rows, 16 * g) for g in range(LANES // 16)], axis=0
            )
            tall = span + taps - half
            hankel = jnp.concatenate([sheet[:, :tall], sheet[:, LANES : LANES + tall]], axis=0)
            product = jnp.dot(stacked, hankel, preferred_element_type=jnp.float32)
            found = product[:tmpl, :span]
            for k in range(1, taps // half):
                found = found + product[k * tmpl : (k + 1) * tmpl, k * half : k * half + span]
            total[seg] += found * level[seg, pl.ds(chan, 1), :] * weight

    unroll = 8

    def body(trip, carry):
        for u in range(unroll):
            one(trip * unroll + u)
        return carry

    lax.fori_loop(0, group // unroll, body, 0)


def correlate(live, base, level, banks, before, first, count, overall):
    segs, chans, _, long = base.shape
    span = level.shape[2]
    per, _, taps = banks[0].shape
    tmpl = per * len(banks)
    at = first // GROUP
    full = (segs, tmpl, span)
    in_specs = [
        SMEM,
        pl.BlockSpec((segs, GROUP, 16, long), lambda i: (0, at + i, 0, 0)),
        pl.BlockSpec((segs, GROUP, span), lambda i: (0, at + i, 0)),
    ]
    for bank in banks:
        skip = at if bank.shape[1] == chans else 0
        in_specs.append(pl.BlockSpec((per, GROUP, taps), lambda i, s=skip: (0, s + i, 0)))
    args = [live, base, level, *banks]
    kernel = functools.partial(corr_kernel, len(banks), first, overall)
    if before is None:
        inner = kernel

        def kernel(live, base, level, *refs):
            inner(live, base, level, *refs[: len(banks)], None, *refs[len(banks) :])
    else:
        in_specs.append(pl.BlockSpec(full, lambda i: (0, 0, 0)))
        args.append(before)
    return pl.pallas_call(
        kernel,
        grid=(count // GROUP,),
        out_shape=jax.ShapeDtypeStruct(full, jnp.float32),
        in_specs=in_specs,
        out_specs=pl.BlockSpec(full, lambda i: (0, 0, 0)),
        scratch_shapes=[pltpu.VMEM((taps // LANES, tmpl * GROUP, LANES), jnp.float32)],
        compiler_params=pltpu.CompilerParams(vmem_limit_bytes=40 * 1024 * 1024),
        cost_estimate=pl.CostEstimate(
            flops=2 * tmpl * count * taps * span * segs,
            bytes_accessed=10**7,
            transcendentals=0,
        ),
    )(*args)


def finish_kernel(counts, rows, *refs):
    parts, (out, both) = refs[:-2], refs[-2:]
    tmpl = parts[0].shape[0]
    start = 0
    for src, count in enumerate(counts):
        value = parts[start][...]
        for ref in parts[start + 1 : start + count]:
            value = value + ref[...]
        both[pl.ds(src * tmpl, tmpl), :] = value
        start += count
    for p in range(out.shape[0]):
        out[pl.ds(p, 1), :] = both[pl.ds(rows[p], 1), :]


def finish(rows, groups):
    parts = [part for group in groups for part in group]
    shape = parts[0].shape
    spec = pl.BlockSpec(shape, lambda i: (0, 0))
    return pl.pallas_call(
        functools.partial(finish_kernel, [len(group) for group in groups]),
        grid=(1,),
        out_shape=jax.ShapeDtypeStruct((rows.shape[0], shape[1]), jnp.float32),
        in_specs=[SMEM] + [spec] * len(parts),
        out_specs=pl.BlockSpec((rows.shape[0], shape[1]), lambda i: (0, 0)),
        scratch_shapes=[pltpu.VMEM((len(groups) * shape[0], shape[1]), jnp.float32)],
        compiler_params=pltpu.CompilerParams(vmem_limit_bytes=40 * 1024 * 1024),
    )(rows, *parts)


def crossed(values, bit):
    return lax.ppermute(values, "tm", [(i, i ^ bit) for i in range(lax.axis_size("tm"))])


def per_device(record, templates, shifts, live_mask, plan):
    count, groups = lax.axis_size("tm"), lax.axis_size("sta")
    per, own_chans, taps = templates.shape
    overall = math.sqrt(taps / (own_chans * groups))
    record, shifts, live_mask = (padded(v, 0, GROUP) for v in (record, shifts, live_mask))
    templates = padded(templates, 1, GROUP)
    chans = record.shape[0]
    far, shared = count // 2, count // 4
    others = [bit for bit in (1 << e for e in range(count.bit_length() - 4, -1, -1))]

    cuts = [0, chans - GROUP, chans] if chans > GROUP else [0, chans]
    spans = list(zip(cuts[:-1], cuts[1:]))
    chunked = {far: [crossed(templates[:, a:b], far) for a, b in spans]}
    whole = {0: templates}
    for bit in others:
        for mask in list(whole):
            whole[mask | bit] = crossed(whole[mask], bit)
        for mask in list(chunked):
            chunked[mask | bit] = [crossed(part, bit) for part in chunked[mask]]

    after = [(i, i - 1) for i in range(1, count)]
    blocks = [
        record,
        lax.ppermute(record, "tm", after),
        crossed(record, shared),
        lax.ppermute(record, "tm", [(i, j ^ shared) for i, j in after]),
    ]
    base, level = prepare(shifts, blocks, taps)

    total = None
    for idx, (a, b) in enumerate(spans):
        banks = list(whole.values()) + [chunked[mask][idx] for mask in chunked]
        total = correlate(live_mask, base, level, banks, total, a, b - a, overall)

    near, away = [total[0]], []
    for by in range(groups):
        if by:
            pairs = [(i, (i + by) % groups) for i in range(groups)]
            near.append(lax.ppermute(total[0], "sta", pairs))
        pairs = [
            (i * count + j, (i + by) % groups * count + (j ^ shared))
            for i in range(groups)
            for j in range(count)
        ]
        away.append(lax.ppermute(total[1], ("sta", "tm"), pairs))

    masks = list(whole) + list(chunked)
    places = np.zeros(count, np.int32)
    for place, mask in enumerate(masks):
        places[mask] = place
        places[mask | shared] = place + len(masks)
    mine = lax.axis_index("tm")
    share = plan.shape[0] // groups
    slots = lax.dynamic_slice_in_dim(plan, lax.axis_index("sta") * share, share)
    rows = jnp.asarray(places)[(slots // per) ^ mine] * per + slots % per
    return finish(rows, [near, away])


def solution(mesh):
    placed = (P("sta", "tm"), P("tm", "sta", None), P("sta"), P("sta"), P())
    return jax.shard_map(
        per_device, mesh=mesh, in_specs=placed, out_specs=P("sta", "tm"), check_vma=False
    )
```

```python
import functools
import math

import jax
import jax.numpy as jnp
import numpy as np
from jax import lax
from jax.experimental import pallas as pl
from jax.experimental.pallas import tpu as pltpu
from jax.sharding import PartitionSpec as P

LANES = 128
GROUP = 16
VMEM_BYTES = 24 * 1024 * 1024
SMEM = pl.BlockSpec(memory_space=pltpu.SMEM)


def rolled_left(values, by):
    width = values.shape[1]
    return pltpu.roll(values, (width - by) % width, 1)


def padded(values, axis, multiple):
    extra = -values.shape[axis] % multiple
    if extra == 0:
        return values
    widths = [(0, extra if i == axis else 0) for i in range(values.ndim)]
    return jnp.pad(values, widths)


def prep_kernel(shifts, *refs):
    segs = len(refs[:-4]) // 2
    blocks, (base, level, lines, flat) = refs[:-4], refs[-4:]
    chans, span = blocks[0].shape
    taps = base.shape[3] - span
    width, long = 2 * span, span + taps
    for seg in range(segs):
        for first in range(0, chans, GROUP):
            part = pl.ds(first, GROUP)
            both = jnp.concatenate(
                [blocks[2 * seg][part, :], blocks[2 * seg + 1][part, :]], axis=1
            ).astype(jnp.float32)
            window, reach = both * both, 1
            while reach < taps:
                window = window + rolled_left(window, reach)
                reach *= 2
            rate = lax.rsqrt(window + 1e-06)
            for m in range(width // LANES):
                cols = slice(m * LANES, (m + 1) * LANES)
                flat[m, pl.ds(8 * first + seg, GROUP, stride=8), :] = both[:, cols]
                flat[m, pl.ds(8 * first + segs + seg, GROUP, stride=8), :] = rate[:, cols]

    flip = 7 - lax.broadcasted_iota(jnp.int32, (8, long), 0)

    def one(chan, slot):
        lag = shifts[chan]
        rows = pl.ds(pl.multiple_of(chan * 8, 8), 8)
        held = jnp.concatenate([flat[m, rows, :] for m in range(width // LANES)], axis=1)
        lines[slot] = pltpu.roll(held, lax.rem(width - lag, width), 1)[:, :long]
        for seg in range(segs):
            level[seg, pl.ds(chan, 1), :] = lines[slot, pl.ds(segs + seg, 1), :span]
            eight = pltpu.roll(
                jnp.broadcast_to(lines[slot, pl.ds(seg, 1), :], (8, long)),
                long - 7,
                1,
                stride=1,
                stride_axis=0,
            )
            eight = jnp.take_along_axis(eight, flip, axis=0, mode="promise_in_bounds")
            base[seg, chan] = jnp.concatenate([eight, rolled_left(eight, 8)], axis=0).astype(
                jnp.bfloat16
            )

    unroll = 4

    def body(step, carry):
        for u in range(unroll):
            one(step * unroll + u, u)
        return carry

    lax.fori_loop(0, chans // unroll, body, 0)


def prepare(shifts, blocks, taps):
    segs = len(blocks) // 2
    chans, span = blocks[0].shape
    whole = [pl.BlockSpec((chans, span), lambda i: (0, 0))] * len(blocks)
    return pl.pallas_call(
        prep_kernel,
        grid=(1,),
        out_shape=[
            jax.ShapeDtypeStruct((segs, chans, 16, span + taps), jnp.bfloat16),
            jax.ShapeDtypeStruct((segs, chans, span), jnp.float32),
        ],
        in_specs=[SMEM] + whole,
        out_specs=[
            pl.BlockSpec((segs, chans, 16, span + taps), lambda i: (0, 0, 0, 0)),
            pl.BlockSpec((segs, chans, span), lambda i: (0, 0, 0)),
        ],
        scratch_shapes=[
            pltpu.VMEM((4, 8, span + taps), jnp.float32),
            pltpu.VMEM((2 * span // LANES, chans * 8, LANES), jnp.float32),
        ],
        compiler_params=pltpu.CompilerParams(vmem_limit_bytes=VMEM_BYTES),
        cost_estimate=pl.CostEstimate(flops=1, bytes_accessed=10**7, transcendentals=0),
    )(shifts, *blocks)


def corr_kernel(pieces, first, overall, live, base, level, *refs):
    banks, (before, total, flat) = refs[:pieces], refs[pieces:]
    per, group, taps = banks[0].shape
    tmpl = per * pieces
    segs, span = level.shape[0], level.shape[2]
    parts, half = taps // LANES, 2 * LANES
    step = pl.program_id(0)

    @pl.when(step == 0)
    def _():
        if before is None:
            total[...] = jnp.zeros_like(total)
        else:
            total[...] = before[...]

    for idx, bank in enumerate(banks):
        rows = bank[...].reshape(per * group, taps).astype(jnp.float32)
        for m in range(parts):
            flat[m, pl.ds(idx * per * group, per * group), :] = rows[
                :, m * LANES : (m + 1) * LANES
            ]

    def one(chan):
        panel = jnp.concatenate(
            [flat[m, pl.ds(chan, tmpl, stride=group), :] for m in range(parts)], axis=1
        )
        power = jnp.sum(panel * panel, axis=1, keepdims=True)
        alive = live[first + step * group + chan].astype(jnp.float32)
        weight = alive * overall * lax.rsqrt(power + 1e-06)
        panel = panel.astype(jnp.bfloat16)
        stacked = jnp.concatenate(
            [panel[:, k * half : (k + 1) * half] for k in range(taps // half)], axis=0
        )
        for seg in range(segs):
            rows = base[seg, chan]
            sheet = jnp.concatenate(
                [rolled_left(rows, 16 * g) for g in range(LANES // 16)], axis=0
            )
            tall = span + taps - half
            hankel = jnp.concatenate([sheet[:, :tall], sheet[:, LANES : LANES + tall]], axis=0)
            product = jnp.dot(stacked, hankel, preferred_element_type=jnp.float32)
            found = product[:tmpl, :span]
            for k in range(1, taps // half):
                found = found + product[k * tmpl : (k + 1) * tmpl, k * half : k * half + span]
            total[seg] += found * level[seg, pl.ds(chan, 1), :] * weight

    unroll = 8

    def body(trip, carry):
        for u in range(unroll):
            one(trip * unroll + u)
        return carry

    lax.fori_loop(0, group // unroll, body, 0)


def correlate(live, base, level, banks, before, first, count, overall, seg=None):
    _, chans, _, long = base.shape
    segs, seg = (base.shape[0], 0) if seg is None else (1, seg)
    span = level.shape[2]
    per, _, taps = banks[0].shape
    tmpl = per * len(banks)
    at = first // GROUP
    full = (segs, tmpl, span)
    in_specs = [
        SMEM,
        pl.BlockSpec((segs, GROUP, 16, long), lambda i: (seg, at + i, 0, 0)),
        pl.BlockSpec((segs, GROUP, span), lambda i: (seg, at + i, 0)),
    ]
    for bank in banks:
        skip = at if bank.shape[1] == chans else 0
        in_specs.append(pl.BlockSpec((per, GROUP, taps), lambda i, s=skip: (0, s + i, 0)))
    args = [live, base, level, *banks]
    kernel = functools.partial(corr_kernel, len(banks), first, overall)
    if before is None:
        inner = kernel

        def kernel(live, base, level, *refs):
            inner(live, base, level, *refs[: len(banks)], None, *refs[len(banks) :])
    else:
        in_specs.append(pl.BlockSpec(full, lambda i: (seg, 0, 0)))
        args.append(before)
    return pl.pallas_call(
        kernel,
        grid=(count // GROUP,),
        out_shape=jax.ShapeDtypeStruct(full, jnp.float32),
        in_specs=in_specs,
        out_specs=pl.BlockSpec(full, lambda i: (0, 0, 0)),
        scratch_shapes=[pltpu.VMEM((taps // LANES, tmpl * GROUP, LANES), jnp.float32)],
        compiler_params=pltpu.CompilerParams(vmem_limit_bytes=VMEM_BYTES),
        cost_estimate=pl.CostEstimate(
            flops=2 * tmpl * count * taps * span * segs,
            bytes_accessed=10**7,
            transcendentals=0,
        ),
    )(*args)


def finish_kernel(counts, per, plan, places, *refs):
    parts, (out, both) = refs[:-2], refs[-2:]
    tmpl, share = parts[0].shape[0], out.shape[0]
    start = 0
    for src, count in enumerate(counts):
        value = parts[start][...]
        for ref in parts[start + 1 : start + count]:
            value = value + ref[...]
        both[pl.ds(src * tmpl, tmpl), :] = value
        start += count
    mine, first = lax.axis_index("tm"), lax.axis_index("sta") * share
    for p in range(share):
        slot = plan[first + p]
        owner = lax.div(slot, per)
        row = places[lax.bitwise_xor(owner, mine)] * per + (slot - owner * per)
        out[pl.ds(p, 1), :] = both[pl.ds(row, 1), :]


def finish(plan, places, per, groups):
    parts = [part for group in groups for part in group]
    tmpl, span = parts[0].shape
    share = plan.shape[0] // lax.axis_size("sta")
    spec = pl.BlockSpec((tmpl, span), lambda i: (0, 0))
    return pl.pallas_call(
        functools.partial(finish_kernel, [len(group) for group in groups], per),
        grid=(1,),
        out_shape=jax.ShapeDtypeStruct((share, span), jnp.float32),
        in_specs=[SMEM] * 2 + [spec] * len(parts),
        out_specs=pl.BlockSpec((share, span), lambda i: (0, 0)),
        scratch_shapes=[pltpu.VMEM((len(groups) * tmpl, span), jnp.float32)],
        compiler_params=pltpu.CompilerParams(vmem_limit_bytes=VMEM_BYTES),
    )(plan, jnp.asarray(places), *parts)


def crossed(values, bit):
    return lax.ppermute(values, "tm", [(i, i ^ bit) for i in range(lax.axis_size("tm"))])


def per_device(record, templates, shifts, live_mask, plan):
    count, groups = lax.axis_size("tm"), lax.axis_size("sta")
    per, own_chans, taps = templates.shape
    overall = math.sqrt(taps / (own_chans * groups))
    record, shifts, live_mask = (padded(v, 0, GROUP) for v in (record, shifts, live_mask))
    templates = padded(templates, 1, GROUP)
    chans = record.shape[0]
    far, shared = count // 2, count // 4
    others = [bit for bit in (1 << e for e in range(count.bit_length() - 4, -1, -1))]

    banks = {0: templates, far: crossed(templates, far)}
    for bit in others[:-1]:
        banks[bit] = crossed(templates, bit)
    after = [(i, i - 1) for i in range(1, count)]
    moved = [
        lax.ppermute(record, "tm", after),
        crossed(record, shared),
        lax.ppermute(record, "tm", [(i, j ^ shared) for i, j in after]),
    ]
    moved, banks[far] = lax.optimization_barrier((moved, banks[far]))
    base, level = prepare(shifts, [record, *moved], taps)
    for bit in others:
        for mask in list(banks):
            if mask | bit not in banks:
                banks[mask | bit] = crossed(banks[mask], bit)
        if bit == others[-2]:
            banks[far | bit], base = lax.optimization_barrier((banks[far | bit], base))
    masks = list(banks)
    total = correlate(
        live_mask, base, level, list(banks.values()), None, 0, chans, overall
    )
    kept, sent = total[0], total[1]

    near, away = [kept], []
    for by in range(groups):
        pairs = [
            (i * count + j, (i + by) % groups * count + (j ^ shared))
            for i in range(groups)
            for j in range(count)
        ]
        away.append(lax.ppermute(sent, ("sta", "tm"), pairs))
    for by in range(1, groups):
        pairs = [(i, (i + by) % groups) for i in range(groups)]
        near.append(lax.ppermute(kept, "sta", pairs))

    places = np.zeros(count, np.int32)
    for place, mask in enumerate(masks):
        places[mask] = place
        places[mask | shared] = place + len(masks)
    return finish(plan, places, per, [near, away])


def solution(mesh):
    placed = (P("sta", "tm"), P("tm", "sta", None), P("sta"), P("sta"), P())
    return jax.shard_map(
        per_device, mesh=mesh, in_specs=placed, out_specs=P("sta", "tm"), check_vma=False
    )
```

```python
import functools
import math

import jax
import jax.numpy as jnp
import numpy as np
from jax import lax
from jax.experimental import pallas as pl
from jax.experimental.pallas import tpu as pltpu
from jax.sharding import PartitionSpec as P

LANES = 128
GROUP = 16
VMEM_BYTES = 24 * 1024 * 1024
SMEM = pl.BlockSpec(memory_space=pltpu.SMEM)
VMEM = pl.BlockSpec(memory_space=pltpu.VMEM)


def rolled_left(values, by):
    width = values.shape[1]
    return pltpu.roll(values, (width - by) % width, 1)


def padded(values, axis, multiple):
    extra = -values.shape[axis] % multiple
    if extra == 0:
        return values
    widths = [(0, extra if i == axis else 0) for i in range(values.ndim)]
    return jnp.pad(values, widths)


def prep_kernel(half, scalars, record, *refs):
    blocks, (base, level, lines, flat, ext) = refs[:-5], refs[-5:]
    segs = (len(blocks) + 1) // 2
    chans, span = record.shape
    kept = base.shape[1]
    taps = base.shape[3] - span
    width, long = 2 * span, span + taps
    start = half() * kept

    sides = (record, *blocks)
    for seg in range(segs):
        for side in range(2):
            ext[seg, :, side * span : (side + 1) * span] = sides[2 * seg + side][...].astype(
                jnp.float32
            )
        for first in range(0, kept, 8):
            both = ext[seg, pl.ds(pl.multiple_of(start + first, 8), 8), :]
            window, reach = both * both, 1
            while reach < taps:
                window = window + rolled_left(window, reach)
                reach *= 2
            rate = lax.rsqrt(window + 1e-06)
            for m in range(width // LANES):
                cols = slice(m * LANES, (m + 1) * LANES)
                flat[m, pl.ds(8 * first + seg, 8, stride=8), :] = both[:, cols]
                flat[m, pl.ds(8 * first + segs + seg, 8, stride=8), :] = rate[:, cols]

    flip = 7 - lax.broadcasted_iota(jnp.int32, (8, long), 0)

    def one(chan, slot):
        lag = scalars[start + chan]
        alive = scalars[chans + start + chan].astype(jnp.float32)
        rows = pl.ds(pl.multiple_of(chan * 8, 8), 8)
        held = jnp.concatenate([flat[m, rows, :] for m in range(width // LANES)], axis=1)
        lines[slot] = pltpu.roll(held, lax.rem(width - lag, width), 1)[:, :long]
        for seg in range(segs):
            level[seg, pl.ds(chan, 1), :] = lines[slot, pl.ds(segs + seg, 1), :span] * alive
            eight = pltpu.roll(
                jnp.broadcast_to(lines[slot, pl.ds(seg, 1), :], (8, long)),
                long - 7,
                1,
                stride=1,
                stride_axis=0,
            )
            eight = jnp.take_along_axis(eight, flip, axis=0, mode="promise_in_bounds")
            base[seg, chan] = jnp.concatenate([eight, rolled_left(eight, 8)], axis=0).astype(
                jnp.bfloat16
            )

    unroll = 4

    def body(step, carry):
        for u in range(unroll):
            one(step * unroll + u, u)
        return carry

    lax.fori_loop(0, kept // unroll, body, 0)


def prepare(half, scalars, record, blocks, taps):
    segs = (len(blocks) + 1) // 2
    chans, span = record.shape
    kept = chans // 2
    return pl.pallas_call(
        functools.partial(prep_kernel, half),
        out_shape=[
            jax.ShapeDtypeStruct((segs, kept, 16, span + taps), jnp.bfloat16),
            jax.ShapeDtypeStruct((segs, kept, span), jnp.float32),
        ],
        in_specs=[SMEM] + [VMEM] * (1 + len(blocks)),
        out_specs=[VMEM] * 2,
        scratch_shapes=[
            pltpu.VMEM((4, 8, span + taps), jnp.float32),
            pltpu.VMEM((2 * span // LANES, kept * 8, LANES), jnp.float32),
            pltpu.VMEM((segs, chans, 2 * span), jnp.float32),
        ],
        compiler_params=pltpu.CompilerParams(vmem_limit_bytes=VMEM_BYTES),
        cost_estimate=pl.CostEstimate(flops=1, bytes_accessed=10**6, transcendentals=0),
    )(scalars, record, *blocks)


def corr_kernel(pieces, groups, overall, per, skip, scalars, base, level, *refs):
    banks, outs, (total, flat) = refs[:pieces], refs[pieces:-2], refs[-2:]
    _, chans, taps = banks[0].shape
    segs, tmpl, span = total.shape
    parts, half = taps // LANES, 2 * LANES

    at = 0
    for bank in banks:
        size = bank.shape[0] * chans
        rows = bank[...].astype(jnp.float32).reshape(size, taps)
        for m in range(parts):
            flat[m, pl.ds(at, size), :] = rows[:, m * LANES : (m + 1) * LANES]
        at += size
    total[...] = jnp.zeros_like(total)

    def one(chan):
        panel = jnp.concatenate(
            [flat[m, pl.ds(chan, tmpl, stride=chans), :] for m in range(parts)], axis=1
        )
        power = jnp.sum(panel * panel, axis=1, keepdims=True)
        weight = overall * lax.rsqrt(power + 1e-06)
        panel = panel.astype(jnp.bfloat16)
        stacked = jnp.concatenate(
            [panel[:, k * half : (k + 1) * half] for k in range(taps // half)], axis=0
        )
        for seg in range(segs):
            rows = base[seg, chan]
            sheet = jnp.concatenate(
                [rolled_left(rows, 16 * g) for g in range(LANES // 16)], axis=0
            )
            tall = span + taps - half
            hankel = jnp.concatenate([sheet[:, :tall], sheet[:, LANES : LANES + tall]], axis=0)
            product = jnp.dot(stacked, hankel, preferred_element_type=jnp.float32)
            found = product[:tmpl, :span]
            for k in range(1, taps // half):
                found = found + product[k * tmpl : (k + 1) * tmpl, k * half : k * half + span]
            total[seg] += found * level[seg, pl.ds(chan, 1), :] * weight

    unroll = 4

    def body(trip, carry):
        for u in range(unroll):
            one(trip * unroll + u)
        return carry

    lax.fori_loop(0, chans // unroll, body, 0)

    share = tmpl // groups
    mine, sta = lax.axis_index("tm"), lax.axis_index("sta")
    for by in range(groups):
        first = lax.rem(sta + by, groups) * share
        for p in range(share):
            slot = scalars[skip + first + p]
            owner = lax.div(slot, per)
            row = scalars[skip + tmpl + lax.bitwise_xor(owner, mine)] + (slot - owner * per)
            for seg in range(segs):
                outs[seg * groups + by][pl.ds(p, 1), :] = total[seg, pl.ds(row, 1), :]


def correlate(per, skip, scalars, base, level, banks, groups, overall):
    segs, chans, span = level.shape
    taps = banks[0].shape[2]
    tmpl = sum(bank.shape[0] for bank in banks)
    count = segs * groups
    return pl.pallas_call(
        functools.partial(corr_kernel, len(banks), groups, overall, per, skip),
        out_shape=[jax.ShapeDtypeStruct((tmpl // groups, span), jnp.float32)] * count,
        in_specs=[SMEM] + [VMEM] * (2 + len(banks)),
        out_specs=[VMEM] * count,
        scratch_shapes=[
            pltpu.VMEM((segs, tmpl, span), jnp.float32),
            pltpu.VMEM((taps // LANES, tmpl * chans, LANES), jnp.float32),
        ],
        compiler_params=pltpu.CompilerParams(vmem_limit_bytes=VMEM_BYTES),
        cost_estimate=pl.CostEstimate(
            flops=2 * tmpl * chans * taps * span * segs, bytes_accessed=10**7, transcendentals=0
        ),
    )(scalars, base, level, *banks)


def crossed(values, bit):
    return lax.ppermute(values, "tm", [(i, i ^ bit) for i in range(lax.axis_size("tm"))])


def per_device(record, templates, shifts, live_mask, plan):
    count, groups = lax.axis_size("tm"), lax.axis_size("sta")
    per, _, taps = templates.shape
    overall = math.sqrt(taps / (record.shape[0] * groups))
    record, shifts, live_mask = (padded(v, 0, GROUP) for v in (record, shifts, live_mask))
    templates = padded(templates, 1, GROUP)
    shared = count // 4
    kept = record.shape[0] // 2

    def half():
        return lax.rem(lax.div(lax.axis_index("tm"), shared), 2)

    mine = lax.dynamic_slice_in_dim(templates, half() * kept, kept, 1)
    other = lax.dynamic_slice_in_dim(templates, (1 - half()) * kept, kept, 1)
    banks = {0: mine}
    for mask in range(count - shared, 0, -shared):
        banks[mask] = crossed(other if mask & shared else mine, mask)
    after = [(i, i - 1) for i in range(1, count)]
    moved = [
        lax.ppermute(record, "tm", after),
        crossed(record, shared),
        lax.ppermute(record, "tm", [(i, j ^ shared) for i, j in after]),
    ]
    bit = shared // 2
    late = [mask for mask in banks if mask & (count // 2)]
    banks[bit] = crossed(mine, bit)
    for mask in [mask for mask in banks if mask not in (0, bit, *late)]:
        banks[mask | bit] = crossed(banks[mask], bit)

    order = list(range(0, count, shared)) + [mask | bit for mask in range(0, count, shared)]
    lower = bit // 2
    while lower:
        order += [mask | lower for mask in order]
        lower //= 2
    places = np.zeros(count, np.int32)
    for place, mask in enumerate(order):
        places[mask] = place * per
    scalars = jnp.concatenate([shifts, live_mask, plan, jnp.asarray(places)])

    *held, moved = lax.optimization_barrier((*(banks[mask] for mask in late), moved))
    banks.update(zip(late, held))
    base, level = prepare(half, scalars, record, moved, taps)
    for mask in late:
        banks[mask | bit] = crossed(banks[mask], bit)
    *pieces, base = lax.optimization_barrier(
        (*(banks[mask] for mask in order if mask in banks), base)
    )
    while bit > 1:
        bit //= 2
        pieces += [crossed(piece, bit) for piece in pieces]

    skip = shifts.shape[0] + live_mask.shape[0]
    stacks = correlate(per, skip, scalars, base, level, pieces, groups, overall)
    total = stacks[0]
    for by in range(groups):
        pairs = [
            (i * count + j, (i + by) % groups * count + (j ^ shared))
            for i in range(groups)
            for j in range(count)
        ]
        total = total + lax.ppermute(stacks[groups + by], ("sta", "tm"), pairs)
        if by:
            pairs = [(i, (i + by) % groups) for i in range(groups)]
            total = total + lax.ppermute(stacks[by], "sta", pairs)
    return total


def solution(mesh):
    placed = (P("sta", "tm"), P("tm", "sta", None), P("sta"), P("sta"), P())
    return jax.shard_map(
        per_device, mesh=mesh, in_specs=placed, out_specs=P("sta", "tm"), check_vma=False
    )
```

```python
import functools
import math

import jax
import jax.numpy as jnp
import numpy as np
from jax import lax
from jax.experimental import pallas as pl
from jax.experimental.pallas import tpu as pltpu
from jax.sharding import PartitionSpec as P

LANES = 128
GROUP = 16
VMEM_BYTES = 24 * 1024 * 1024
SMEM = pl.BlockSpec(memory_space=pltpu.SMEM)
VMEM = pl.BlockSpec(memory_space=pltpu.VMEM)


def rolled_left(values, by):
    width = values.shape[1]
    return pltpu.roll(values, (width - by) % width, 1)


def padded(values, axis, multiple):
    extra = -values.shape[axis] % multiple
    if extra == 0:
        return values
    widths = [(0, extra if i == axis else 0) for i in range(values.ndim)]
    return jnp.pad(values, widths)


def prep_kernel(half, scalars, record, *refs):
    blocks, (base, level, lines, flat, ext) = refs[:-5], refs[-5:]
    segs = len(blocks)
    chans, span = record.shape
    kept = base.shape[1]
    taps = base.shape[3] - span
    width, long = 2 * span, span + taps
    start = half() * kept

    rim, *others = blocks
    for side, block in enumerate((record, rim)):
        ext[:, side * span : (side + 1) * span] = block[...].astype(jnp.float32)
    for seg in range(segs):
        for first in range(0, kept, 8):
            if seg == 0:
                both = ext[pl.ds(pl.multiple_of(start + first, 8), 8), :]
            else:
                both = others[seg - 1][...].astype(jnp.float32)[first : first + 8, :]
            window, reach = both * both, 1
            while reach < taps:
                window = window + rolled_left(window, reach)
                reach *= 2
            rate = lax.rsqrt(window + 1e-06)
            for m in range(width // LANES):
                cols = slice(m * LANES, (m + 1) * LANES)
                flat[m, pl.ds(8 * first + seg, 8, stride=8), :] = both[:, cols]
                flat[m, pl.ds(8 * first + segs + seg, 8, stride=8), :] = rate[:, cols]

    flip = 7 - lax.broadcasted_iota(jnp.int32, (8, long), 0)

    def one(chan, slot):
        lag = scalars[start + chan]
        alive = scalars[chans + start + chan].astype(jnp.float32)
        rows = pl.ds(pl.multiple_of(chan * 8, 8), 8)
        held = jnp.concatenate([flat[m, rows, :] for m in range(width // LANES)], axis=1)
        lines[slot] = pltpu.roll(held, lax.rem(width - lag, width), 1)[:, :long]
        for seg in range(segs):
            level[seg, pl.ds(chan, 1), :] = lines[slot, pl.ds(segs + seg, 1), :span] * alive
            eight = pltpu.roll(
                jnp.broadcast_to(lines[slot, pl.ds(seg, 1), :], (8, long)),
                long - 7,
                1,
                stride=1,
                stride_axis=0,
            )
            eight = jnp.take_along_axis(eight, flip, axis=0, mode="promise_in_bounds")
            base[seg, chan] = jnp.concatenate([eight, rolled_left(eight, 8)], axis=0).astype(
                jnp.bfloat16
            )

    unroll = 4

    def body(step, carry):
        for u in range(unroll):
            one(step * unroll + u, u)
        return carry

    lax.fori_loop(0, kept // unroll, body, 0)


def prepare(half, scalars, record, blocks, taps):
    segs = len(blocks)
    chans, span = record.shape
    kept = chans // 2
    return pl.pallas_call(
        functools.partial(prep_kernel, half),
        out_shape=[
            jax.ShapeDtypeStruct((segs, kept, 16, span + taps), jnp.bfloat16),
            jax.ShapeDtypeStruct((segs, kept, span), jnp.float32),
        ],
        in_specs=[SMEM] + [VMEM] * (1 + len(blocks)),
        out_specs=[VMEM] * 2,
        scratch_shapes=[
            pltpu.VMEM((4, 8, span + taps), jnp.float32),
            pltpu.VMEM((2 * span // LANES, kept * 8, LANES), jnp.float32),
            pltpu.VMEM((chans, 2 * span), jnp.float32),
        ],
        compiler_params=pltpu.CompilerParams(vmem_limit_bytes=VMEM_BYTES),
        cost_estimate=pl.CostEstimate(flops=1, bytes_accessed=10**6, transcendentals=0),
    )(scalars, record, *blocks)


def corr_kernel(pieces, groups, overall, per, skip, scalars, base, level, *refs):
    banks, outs, (total, flat) = refs[:pieces], refs[pieces:-2], refs[-2:]
    _, chans, taps = banks[0].shape
    segs, tmpl, span = total.shape
    parts, half = taps // LANES, 2 * LANES

    at = 0
    for bank in banks:
        size = bank.shape[0] * chans
        rows = bank[...].astype(jnp.float32).reshape(size, taps)
        for m in range(parts):
            flat[m, pl.ds(at, size), :] = rows[:, m * LANES : (m + 1) * LANES]
        at += size
    total[...] = jnp.zeros_like(total)

    def one(chan):
        panel = jnp.concatenate(
            [flat[m, pl.ds(chan, tmpl, stride=chans), :] for m in range(parts)], axis=1
        )
        power = jnp.sum(panel * panel, axis=1, keepdims=True)
        weight = overall * lax.rsqrt(power + 1e-06)
        panel = panel.astype(jnp.bfloat16)
        stacked = jnp.concatenate(
            [panel[:, k * half : (k + 1) * half] for k in range(taps // half)], axis=0
        )
        for seg in range(segs):
            rows = base[seg, chan]
            sheet = jnp.concatenate(
                [rolled_left(rows, 16 * g) for g in range(LANES // 16)], axis=0
            )
            tall = span + taps - half
            hankel = jnp.concatenate([sheet[:, :tall], sheet[:, LANES : LANES + tall]], axis=0)
            product = jnp.dot(stacked, hankel, preferred_element_type=jnp.float32)
            found = product[:tmpl, :span]
            for k in range(1, taps // half):
                found = found + product[k * tmpl : (k + 1) * tmpl, k * half : k * half + span]
            total[seg] += found * level[seg, pl.ds(chan, 1), :] * weight

    unroll = math.gcd(chans, 8)

    def body(trip, carry):
        for u in range(unroll):
            one(trip * unroll + u)
        return carry

    lax.fori_loop(0, chans // unroll, body, 0)

    share = tmpl // groups
    mine, sta = lax.axis_index("tm"), lax.axis_index("sta")
    for by in range(groups):
        first = lax.rem(sta + by, groups) * share
        for p in range(share):
            slot = scalars[skip + first + p]
            owner = lax.div(slot, per)
            row = scalars[skip + tmpl + lax.bitwise_xor(owner, mine)] + (slot - owner * per)
            for seg in range(segs):
                outs[seg * groups + by][pl.ds(p, 1), :] = total[seg, pl.ds(row, 1), :]


def correlate(per, skip, scalars, base, level, banks, groups, overall):
    segs, chans, span = level.shape
    taps = banks[0].shape[2]
    tmpl = sum(bank.shape[0] for bank in banks)
    count = segs * groups
    return pl.pallas_call(
        functools.partial(corr_kernel, len(banks), groups, overall, per, skip),
        out_shape=[jax.ShapeDtypeStruct((tmpl // groups, span), jnp.float32)] * count,
        in_specs=[SMEM] + [VMEM] * (2 + len(banks)),
        out_specs=[VMEM] * count,
        scratch_shapes=[
            pltpu.VMEM((segs, tmpl, span), jnp.float32),
            pltpu.VMEM((taps // LANES, tmpl * chans, LANES), jnp.float32),
        ],
        compiler_params=pltpu.CompilerParams(vmem_limit_bytes=VMEM_BYTES),
        cost_estimate=pl.CostEstimate(
            flops=2 * tmpl * chans * taps * span * segs, bytes_accessed=10**7, transcendentals=0
        ),
    )(scalars, base, level, *banks)


def crossed(values, bit):
    return lax.ppermute(values, "tm", [(i, i ^ bit) for i in range(lax.axis_size("tm"))])


def per_device(record, templates, shifts, live_mask, plan):
    count, groups = lax.axis_size("tm"), lax.axis_size("sta")
    per, _, taps = templates.shape
    overall = math.sqrt(taps / (record.shape[0] * groups))
    record, shifts, live_mask = (padded(v, 0, GROUP) for v in (record, shifts, live_mask))
    templates = padded(templates, 1, GROUP)
    shared = count // 4
    kept = record.shape[0] // 2

    def half():
        return lax.rem(lax.div(lax.axis_index("tm"), shared), 2)

    mine = lax.dynamic_slice_in_dim(templates, half() * kept, kept, 1)
    other = lax.dynamic_slice_in_dim(templates, (1 - half()) * kept, kept, 1)
    banks = {0: mine}
    for mask in range(count - shared, 0, -shared):
        banks[mask] = crossed(other if mask & shared else mine, mask)
    after = [(i, i - 1) for i in range(1, count)]
    rim = lax.ppermute(record, "tm", after)
    given = jnp.concatenate(
        [lax.dynamic_slice_in_dim(v, (1 - half()) * kept, kept, 0) for v in (record, rim)], axis=1
    )
    moved = [rim, crossed(given, shared)]
    bit = shared // 2
    late = [mask for mask in banks if mask & (count // 2)]
    banks[bit] = crossed(mine, bit)
    for mask in [mask for mask in banks if mask not in (0, bit, *late)]:
        banks[mask | bit] = crossed(banks[mask], bit)

    order = list(range(0, count, shared)) + [mask | bit for mask in range(0, count, shared)]
    lower = bit // 2
    while lower:
        order += [mask | lower for mask in order]
        lower //= 2
    places = np.zeros(count, np.int32)
    for place, mask in enumerate(order):
        places[mask] = place * per
    scalars = jnp.concatenate([shifts, live_mask, plan, jnp.asarray(places)])

    base, level = prepare(half, scalars, record, moved, taps)
    for mask in late:
        banks[mask | bit] = crossed(banks[mask], bit)
    *pieces, base = lax.optimization_barrier(
        (*(banks[mask] for mask in order if mask in banks), base)
    )
    while bit > 1:
        bit //= 2
        pieces += [crossed(piece, bit) for piece in pieces]

    skip = shifts.shape[0] + live_mask.shape[0]
    stacks = correlate(per, skip, scalars, base, level, pieces, groups, overall)
    total = stacks[0]
    for by in range(groups):
        pairs = [
            (i * count + j, (i + by) % groups * count + (j ^ shared))
            for i in range(groups)
            for j in range(count)
        ]
        total = total + lax.ppermute(stacks[groups + by], ("sta", "tm"), pairs)
        if by:
            pairs = [(i, (i + by) % groups) for i in range(groups)]
            total = total + lax.ppermute(stacks[by], "sta", pairs)
    return total


def solution(mesh):
    placed = (P("sta", "tm"), P("tm", "sta", None), P("sta"), P("sta"), P())
    return jax.shard_map(
        per_device, mesh=mesh, in_specs=placed, out_specs=P("sta", "tm"), check_vma=False
    )
```

```python
import functools
import math

import jax
import jax.numpy as jnp
import numpy as np
from jax import lax
from jax.experimental import pallas as pl
from jax.experimental.pallas import tpu as pltpu
from jax.sharding import PartitionSpec as P

LANES = 128
GROUP = 16
VMEM_BYTES = 24 * 1024 * 1024
SMEM = pl.BlockSpec(memory_space=pltpu.SMEM)
VMEM = pl.BlockSpec(memory_space=pltpu.VMEM)


def rolled_left(values, by):
    width = values.shape[1]
    return pltpu.roll(values, (width - by) % width, 1)


def padded(values, axis, multiple):
    extra = -values.shape[axis] % multiple
    if extra == 0:
        return values
    widths = [(0, extra if i == axis else 0) for i in range(values.ndim)]
    return jnp.pad(values, widths)


def prep_kernel(half, chans, scalars, *refs):
    blocks, (base, level, lines, flat) = refs[:-4], refs[-4:]
    segs, kept, _, long = base.shape
    span = level.shape[2]
    taps, width = long - span, 2 * span
    start = half() * kept

    for seg, block in enumerate(blocks):
        whole = block[...].astype(jnp.float32)
        for first in range(0, kept, 8):
            both = whole[first : first + 8, :]
            window, reach = both * both, 1
            while reach < taps:
                window = window + rolled_left(window, reach)
                reach *= 2
            rate = lax.rsqrt(window + 1e-06)
            for m in range(width // LANES):
                cols = slice(m * LANES, (m + 1) * LANES)
                flat[m, pl.ds(8 * first + seg, 8, stride=8), :] = both[:, cols]
                flat[m, pl.ds(8 * first + segs + seg, 8, stride=8), :] = rate[:, cols]

    flip = 7 - lax.broadcasted_iota(jnp.int32, (8, long), 0)

    def one(chan, slot):
        lag = scalars[start + chan]
        alive = scalars[chans + start + chan].astype(jnp.float32)
        rows = pl.ds(pl.multiple_of(chan * 8, 8), 8)
        held = jnp.concatenate([flat[m, rows, :] for m in range(width // LANES)], axis=1)
        lines[slot] = pltpu.roll(held, lax.rem(width - lag, width), 1)[:, :long]
        for seg in range(segs):
            level[seg, pl.ds(chan, 1), :] = lines[slot, pl.ds(segs + seg, 1), :span] * alive
            eight = pltpu.roll(
                jnp.broadcast_to(lines[slot, pl.ds(seg, 1), :], (8, long)),
                long - 7,
                1,
                stride=1,
                stride_axis=0,
            )
            eight = jnp.take_along_axis(eight, flip, axis=0, mode="promise_in_bounds")
            base[seg, chan] = jnp.concatenate([eight, rolled_left(eight, 8)], axis=0).astype(
                jnp.bfloat16
            )

    unroll = 4

    def body(step, carry):
        for u in range(unroll):
            one(step * unroll + u, u)
        return carry

    lax.fori_loop(0, kept // unroll, body, 0)


def prepare(half, chans, scalars, blocks, taps):
    segs = len(blocks)
    kept, width = blocks[0].shape
    span = width // 2
    return pl.pallas_call(
        functools.partial(prep_kernel, half, chans),
        out_shape=[
            jax.ShapeDtypeStruct((segs, kept, 16, span + taps), jnp.bfloat16),
            jax.ShapeDtypeStruct((segs, kept, span), jnp.float32),
        ],
        in_specs=[SMEM] + [VMEM] * segs,
        out_specs=[VMEM] * 2,
        scratch_shapes=[
            pltpu.VMEM((8, 8, span + taps), jnp.float32),
            pltpu.VMEM((width // LANES, kept * 8, LANES), jnp.float32),
        ],
        compiler_params=pltpu.CompilerParams(vmem_limit_bytes=VMEM_BYTES),
        cost_estimate=pl.CostEstimate(flops=1, bytes_accessed=10**6, transcendentals=0),
    )(scalars, *blocks)


def corr_kernel(pieces, groups, overall, per, skip, scalars, base, level, *refs):
    banks, outs, (total, flat) = refs[:pieces], refs[pieces:-2], refs[-2:]
    _, chans, taps = banks[0].shape
    segs, tmpl, span = total.shape
    parts, half = taps // LANES, 2 * LANES

    at = 0
    for bank in banks:
        size = bank.shape[0] * chans
        rows = bank[...].astype(jnp.float32).reshape(size, taps)
        for m in range(parts):
            flat[m, pl.ds(at, size), :] = rows[:, m * LANES : (m + 1) * LANES]
        at += size
    total[...] = jnp.zeros_like(total)

    def one(chan):
        panel = jnp.concatenate(
            [flat[m, pl.ds(chan, tmpl, stride=chans), :] for m in range(parts)], axis=1
        )
        power = jnp.sum(panel * panel, axis=1, keepdims=True)
        weight = overall * lax.rsqrt(power + 1e-06)
        panel = panel.astype(jnp.bfloat16)
        stacked = jnp.concatenate(
            [panel[:, k * half : (k + 1) * half] for k in range(taps // half)], axis=0
        )
        for seg in range(segs):
            rows = base[seg, chan]
            sheet = jnp.concatenate(
                [rolled_left(rows, 16 * g) for g in range(LANES // 16)], axis=0
            )
            tall = span + taps - half
            hankel = jnp.concatenate([sheet[:, :tall], sheet[:, LANES : LANES + tall]], axis=0)
            product = jnp.dot(stacked, hankel, preferred_element_type=jnp.float32)
            found = product[:tmpl, :span]
            for k in range(1, taps // half):
                found = found + product[k * tmpl : (k + 1) * tmpl, k * half : k * half + span]
            total[seg] += found * level[seg, pl.ds(chan, 1), :] * weight

    unroll = math.gcd(chans, 8)

    def body(trip, carry):
        for u in range(unroll):
            one(trip * unroll + u)
        return carry

    lax.fori_loop(0, chans // unroll, body, 0)

    share = tmpl // groups
    mine, sta = lax.axis_index("tm"), lax.axis_index("sta")
    for by in range(groups):
        first = lax.rem(sta + by, groups) * share
        for p in range(share):
            slot = scalars[skip + first + p]
            owner = lax.div(slot, per)
            row = scalars[skip + tmpl + lax.bitwise_xor(owner, mine)] + (slot - owner * per)
            for seg in range(segs):
                outs[seg * groups + by][pl.ds(p, 1), :] = total[seg, pl.ds(row, 1), :]


def correlate(per, skip, scalars, base, level, banks, groups, overall):
    segs, chans, span = level.shape
    taps = banks[0].shape[2]
    tmpl = sum(bank.shape[0] for bank in banks)
    count = segs * groups
    return pl.pallas_call(
        functools.partial(corr_kernel, len(banks), groups, overall, per, skip),
        out_shape=[jax.ShapeDtypeStruct((tmpl // groups, span), jnp.float32)] * count,
        in_specs=[SMEM] + [VMEM] * (2 + len(banks)),
        out_specs=[VMEM] * count,
        scratch_shapes=[
            pltpu.VMEM((segs, tmpl, span), jnp.float32),
            pltpu.VMEM((taps // LANES, tmpl * chans, LANES), jnp.float32),
        ],
        compiler_params=pltpu.CompilerParams(vmem_limit_bytes=VMEM_BYTES),
        cost_estimate=pl.CostEstimate(
            flops=2 * tmpl * chans * taps * span * segs, bytes_accessed=10**7, transcendentals=0
        ),
    )(scalars, base, level, *banks)


def crossed(values, bit):
    return lax.ppermute(values, "tm", [(i, i ^ bit) for i in range(lax.axis_size("tm"))])


def per_device(record, templates, shifts, live_mask, plan):
    count, groups = lax.axis_size("tm"), lax.axis_size("sta")
    per, _, taps = templates.shape
    overall = math.sqrt(taps / (record.shape[0] * groups))
    record, shifts, live_mask = (padded(v, 0, GROUP) for v in (record, shifts, live_mask))
    templates = padded(templates, 1, GROUP)
    shared = count // 4
    kept = record.shape[0] // 2

    def half():
        return lax.rem(lax.div(lax.axis_index("tm"), shared), 2)

    mine = lax.dynamic_slice_in_dim(templates, half() * kept, kept, 1)
    other = lax.dynamic_slice_in_dim(templates, (1 - half()) * kept, kept, 1)
    banks = {0: mine}
    for mask in range(count - shared, 0, -shared):
        banks[mask] = crossed(other if mask & shared else mine, mask)
    after = [(i, i - 1) for i in range(1, count)]
    rim = lax.ppermute(record, "tm", after)

    def joined(part):
        return jnp.concatenate(
            [lax.dynamic_slice_in_dim(v, part * kept, kept, 0) for v in (record, rim)], axis=1
        )

    given, own = joined(1 - half()), joined(half())
    moved = [own, crossed(given, shared)]
    bit = shared // 2
    late = [mask for mask in banks if mask & (count // 2)]
    banks[bit] = crossed(mine, bit)
    for mask in [mask for mask in banks if mask not in (0, bit, *late)]:
        banks[mask | bit] = crossed(banks[mask], bit)

    order = list(range(0, count, shared)) + [mask | bit for mask in range(0, count, shared)]
    lower = bit // 2
    while lower:
        order += [mask | lower for mask in order]
        lower //= 2
    places = np.zeros(count, np.int32)
    for place, mask in enumerate(order):
        places[mask] = place * per
    scalars = jnp.concatenate([shifts, live_mask, plan, jnp.asarray(places)])

    base, level = prepare(half, record.shape[0], scalars, moved, taps)
    for mask in late:
        banks[mask | bit] = crossed(banks[mask], bit)
    last = [mask | bit for mask in range(shared, count, shared)]
    soon = [mask for mask in banks if mask not in last]
    *held, base = lax.optimization_barrier((*(banks[mask] for mask in soon), base))
    banks.update(zip(soon, held))
    *held, base = lax.optimization_barrier((*(banks[mask] for mask in last), base))
    banks.update(zip(last, held))
    pieces = [banks[mask] for mask in order if mask in banks]
    while bit > 1:
        bit //= 2
        pieces += [crossed(piece, bit) for piece in pieces]

    skip = shifts.shape[0] + live_mask.shape[0]
    stacks = correlate(per, skip, scalars, base, level, pieces, groups, overall)
    total = stacks[0]
    for by in range(groups):
        pairs = [
            (i * count + j, (i + by) % groups * count + (j ^ shared))
            for i in range(groups)
            for j in range(count)
        ]
        total = total + lax.ppermute(stacks[groups + by], ("sta", "tm"), pairs)
        if by:
            pairs = [(i, (i + by) % groups) for i in range(groups)]
            total = total + lax.ppermute(stacks[by], "sta", pairs)
    return total


def solution(mesh):
    placed = (P("sta", "tm"), P("tm", "sta", None), P("sta"), P("sta"), P())
    return jax.shard_map(
        per_device, mesh=mesh, in_specs=placed, out_specs=P("sta", "tm"), check_vma=False
    )
```

```python
import functools
import math

import jax
import jax.numpy as jnp
import numpy as np
from jax import lax
from jax.experimental import pallas as pl
from jax.experimental.pallas import tpu as pltpu
from jax.sharding import PartitionSpec as P

LANES = 128
GROUP = 16
VMEM_BYTES = 24 * 1024 * 1024
SMEM = pl.BlockSpec(memory_space=pltpu.SMEM)
VMEM = pl.BlockSpec(memory_space=pltpu.VMEM)


def rolled_left(values, by):
    width = values.shape[1]
    return pltpu.roll(values, (width - by) % width, 1)


def padded(values, axis, multiple):
    extra = -values.shape[axis] % multiple
    if extra == 0:
        return values
    widths = [(0, extra if i == axis else 0) for i in range(values.ndim)]
    return jnp.pad(values, widths)


def prep_kernel(half, chans, scalars, *refs):
    blocks, (base, level, lines, flat) = refs[:-4], refs[-4:]
    segs, kept, _, long = base.shape
    span = level.shape[2]
    taps, width = long - span, 2 * span
    start = half() * kept

    for seg, block in enumerate(blocks):
        whole = block[...].astype(jnp.float32)
        for first in range(0, kept, 8):
            both = whole[first : first + 8, :]
            window, reach = both * both, 1
            while reach < taps:
                window = window + rolled_left(window, reach)
                reach *= 2
            rate = lax.rsqrt(window + 1e-06)
            for m in range(width // LANES):
                cols = slice(m * LANES, (m + 1) * LANES)
                flat[m, pl.ds(8 * first + seg, 8, stride=8), :] = both[:, cols]
                flat[m, pl.ds(8 * first + segs + seg, 8, stride=8), :] = rate[:, cols]

    flip = 7 - lax.broadcasted_iota(jnp.int32, (8, long), 0)

    def one(chan, slot):
        lag = scalars[start + chan]
        alive = scalars[chans + start + chan].astype(jnp.float32)
        rows = pl.ds(pl.multiple_of(chan * 8, 8), 8)
        held = jnp.concatenate([flat[m, rows, :] for m in range(width // LANES)], axis=1)
        lines[slot] = pltpu.roll(held, lax.rem(width - lag, width), 1)[:, :long]
        for seg in range(segs):
            level[seg, pl.ds(chan, 1), :] = lines[slot, pl.ds(segs + seg, 1), :span] * alive
            eight = pltpu.roll(
                jnp.broadcast_to(lines[slot, pl.ds(seg, 1), :], (8, long)),
                long - 7,
                1,
                stride=1,
                stride_axis=0,
            )
            eight = jnp.take_along_axis(eight, flip, axis=0, mode="promise_in_bounds")
            base[seg, chan] = jnp.concatenate([eight, rolled_left(eight, 8)], axis=0).astype(
                jnp.bfloat16
            )

    unroll = 4

    def body(step, carry):
        for u in range(unroll):
            one(step * unroll + u, u)
        return carry

    lax.fori_loop(0, kept // unroll, body, 0)


def prepare(half, chans, scalars, blocks, taps):
    segs = len(blocks)
    kept, width = blocks[0].shape
    span = width // 2
    return pl.pallas_call(
        functools.partial(prep_kernel, half, chans),
        out_shape=[
            jax.ShapeDtypeStruct((segs, kept, 16, span + taps), jnp.bfloat16),
            jax.ShapeDtypeStruct((segs, kept, span), jnp.float32),
        ],
        in_specs=[SMEM] + [VMEM] * segs,
        out_specs=[VMEM] * 2,
        scratch_shapes=[
            pltpu.VMEM((8, 8, span + taps), jnp.float32),
            pltpu.VMEM((width // LANES, (kept + 1) * 8, LANES), jnp.float32),
        ],
        compiler_params=pltpu.CompilerParams(vmem_limit_bytes=VMEM_BYTES),
        cost_estimate=pl.CostEstimate(flops=1, bytes_accessed=10**6, transcendentals=0),
    )(scalars, *blocks)


def corr_kernel(pieces, groups, overall, per, skip, scalars, base, level, *refs):
    banks, outs, (total, flat) = refs[:pieces], refs[pieces:-2], refs[-2:]
    _, chans, taps = banks[0].shape
    segs, tmpl, span = total.shape
    parts, half = taps // LANES, 2 * LANES

    at = 0
    for bank in banks:
        size = bank.shape[0] * chans
        rows = bank[...].astype(jnp.float32).reshape(size, taps)
        for m in range(parts):
            flat[m, pl.ds(at, size), :] = rows[:, m * LANES : (m + 1) * LANES]
        at += size
    total[...] = jnp.zeros_like(total)

    def one(chan):
        panel = jnp.concatenate(
            [flat[m, pl.ds(chan, tmpl, stride=chans), :] for m in range(parts)], axis=1
        )
        power = jnp.sum(panel * panel, axis=1, keepdims=True)
        weight = overall * lax.rsqrt(power + 1e-06)
        panel = panel.astype(jnp.bfloat16)
        stacked = jnp.concatenate(
            [panel[:, k * half : (k + 1) * half] for k in range(taps // half)], axis=0
        )
        for seg in range(segs):
            rows = base[seg, chan]
            sheet = jnp.concatenate(
                [rolled_left(rows, 16 * g) for g in range(LANES // 16)], axis=0
            )
            tall = span + taps - half
            hankel = jnp.concatenate([sheet[:, :tall], sheet[:, LANES : LANES + tall]], axis=0)
            product = jnp.dot(stacked, hankel, preferred_element_type=jnp.float32)
            found = product[:tmpl, :span]
            for k in range(1, taps // half):
                found = found + product[k * tmpl : (k + 1) * tmpl, k * half : k * half + span]
            total[seg] += found * level[seg, pl.ds(chan, 1), :] * weight

    unroll = math.gcd(chans, 8)

    def body(trip, carry):
        for u in range(unroll):
            one(trip * unroll + u)
        return carry

    lax.fori_loop(0, chans // unroll, body, 0)

    share = tmpl // groups
    mine, sta = lax.axis_index("tm"), lax.axis_index("sta")
    for by in range(groups):
        first = lax.rem(sta + by, groups) * share
        for p in range(share):
            slot = scalars[skip + first + p]
            owner = lax.div(slot, per)
            row = scalars[skip + tmpl + lax.bitwise_xor(owner, mine)] + (slot - owner * per)
            for seg in range(segs):
                outs[seg * groups + by][pl.ds(p, 1), :] = total[seg, pl.ds(row, 1), :]


def correlate(per, skip, scalars, base, level, banks, groups, overall):
    segs, chans, span = level.shape
    taps = banks[0].shape[2]
    tmpl = sum(bank.shape[0] for bank in banks)
    count = segs * groups
    return pl.pallas_call(
        functools.partial(corr_kernel, len(banks), groups, overall, per, skip),
        out_shape=[jax.ShapeDtypeStruct((tmpl // groups, span), jnp.float32)] * count,
        in_specs=[SMEM] + [VMEM] * (2 + len(banks)),
        out_specs=[VMEM] * count,
        scratch_shapes=[
            pltpu.VMEM((segs, tmpl, span), jnp.float32),
            pltpu.VMEM((taps // LANES, (tmpl + 1) * chans, LANES), jnp.float32),
        ],
        compiler_params=pltpu.CompilerParams(vmem_limit_bytes=VMEM_BYTES),
        cost_estimate=pl.CostEstimate(
            flops=2 * tmpl * chans * taps * span * segs, bytes_accessed=10**7, transcendentals=0
        ),
    )(scalars, base, level, *banks)


def crossed(values, bit):
    return lax.ppermute(values, "tm", [(i, i ^ bit) for i in range(lax.axis_size("tm"))])


def per_device(record, templates, shifts, live_mask, plan):
    count, groups = lax.axis_size("tm"), lax.axis_size("sta")
    per, _, taps = templates.shape
    overall = math.sqrt(taps / (record.shape[0] * groups))
    record, shifts, live_mask = (padded(v, 0, GROUP) for v in (record, shifts, live_mask))
    templates = padded(templates, 1, GROUP)
    shared = count // 4
    kept = record.shape[0] // 2

    def half():
        return lax.rem(lax.div(lax.axis_index("tm"), shared), 2)

    mine = lax.dynamic_slice_in_dim(templates, half() * kept, kept, 1)
    other = lax.dynamic_slice_in_dim(templates, (1 - half()) * kept, kept, 1)
    banks = {0: mine}
    for mask in range(count - shared, 0, -shared):
        banks[mask] = crossed(other if mask & shared else mine, mask)
    after = [(i, i - 1) for i in range(1, count)]
    rim = lax.ppermute(record, "tm", after)

    def joined(part):
        return jnp.concatenate(
            [lax.dynamic_slice_in_dim(v, part * kept, kept, 0) for v in (record, rim)], axis=1
        )

    given, own = joined(1 - half()), joined(half())
    moved = [own, crossed(given, shared)]
    bit = shared // 2
    late = [mask for mask in banks if mask & (count // 2)]
    banks[bit] = crossed(mine, bit)
    for mask in [mask for mask in banks if mask not in (0, bit, *late)]:
        banks[mask | bit] = crossed(banks[mask], bit)

    order = list(range(0, count, shared)) + [mask | bit for mask in range(0, count, shared)]
    lower = bit // 2
    while lower:
        order += [mask | lower for mask in order]
        lower //= 2
    places = np.zeros(count, np.int32)
    for place, mask in enumerate(order):
        places[mask] = place * per
    scalars = jnp.concatenate([shifts, live_mask, plan, jnp.asarray(places)])

    base, level = prepare(half, record.shape[0], scalars, moved, taps)
    for mask in late:
        banks[mask | bit] = crossed(banks[mask], bit)
    last = [mask | bit for mask in range(shared, count, shared)]
    soon = [mask for mask in banks if mask not in last]
    *held, base = lax.optimization_barrier((*(banks[mask] for mask in soon), base))
    banks.update(zip(soon, held))
    *held, base = lax.optimization_barrier((*(banks[mask] for mask in last), base))
    banks.update(zip(last, held))
    pieces = [banks[mask] for mask in order if mask in banks]
    while bit > 1:
        bit //= 2
        pieces += [crossed(piece, bit) for piece in pieces]

    skip = shifts.shape[0] + live_mask.shape[0]
    stacks = correlate(per, skip, scalars, base, level, pieces, groups, overall)
    found = []
    for by in range(groups):
        if by:
            pairs = [(i, (i + by) % groups) for i in range(groups)]
            found.append(lax.ppermute(stacks[by], "sta", pairs))
    for by in range(groups):
        pairs = [
            (i * count + j, (i + by) % groups * count + (j ^ shared))
            for i in range(groups)
            for j in range(count)
        ]
        found.append(lax.ppermute(stacks[groups + by], ("sta", "tm"), pairs))
    total = stacks[0]
    for part in found:
        total = total + part
    return total


def solution(mesh):
    placed = (P("sta", "tm"), P("tm", "sta", None), P("sta"), P("sta"), P())
    return jax.shard_map(
        per_device, mesh=mesh, in_specs=placed, out_specs=P("sta", "tm"), check_vma=False
    )
```
